32 devices in a mesh: grp: 2 (over y), row: 8 (over z, x), tile: 2 (over core).
Axes of the slice: x: 2, y: 2, z: 4, core: 2. Of those that a mesh axis runs over, the one named last changes fastest.
Arguments:
- right_side: bfloat16 [16, 4096, 384], P(('grp', 'row'), 'tile'), parts along dimension 0, may hold values from -6 to 6
- diag_inverse: bfloat16 [3, 4096, 4096], P(None, ('row', 'tile')), may hold values from -0.09375 to 0.09375
- u_factor: bfloat16 [8, 3, 4096, 384], P('row', None, 'tile'), may hold values from -0.5 to 0.5
- v_factor: bfloat16 [8, 3, 4096, 384], P('row', None, 'tile'), may hold values from -0.09375 to 0.09375
- ranks: int32 [8, 3], P('row'), may hold values from 64 to 384, as said below
- pivots: int32 [3], replicated, may hold values from 0 to 7, as said below
Outputs:
- solution: bfloat16 [3, 8192, 384], P(None, ('grp', 'row', 'tile')), parts along dimension 1
- residual_out: float32 [16, 4096, 384], P(('grp', 'row'), 'tile'), parts along dimension 0
The draws below stay inside these ranges and needn't reach their ends.
There are 2 independent parts, one for each index of `grp`. The reference program is written for one: setup_inputs(seed, part) draws one part's arguments, and reference() takes and returns one part's arrays. A program takes and returns all parts, laid end to end along the dimension named above; an argument that names none is the same for every part. Nothing has to cross between parts.
Inputs may be any that keep to these rules, and one draw needn't show every extreme that they name: `ranks`: each entry is 384 // 6 times one of 1, 2, 3, 4, 6; in every draw some block row has rank 384 in every pivot column. `pivots`: distinct block rows of the strip; the first and the last block row are always among them, in an order drawn from the seed.
All inputs are finite; a program needn't handle non-finite values.
Results may differ from the reference program's by a relative error of at most 0.0085.
Values may be sent and summed in bfloat16 or wider, within the bound.
A program may use at most 64 MiB of HBM per device.

```python
import jax
import jax.numpy as jnp
from jax import lax

BS = 4096
RMAX = 384
RHS = 384
PIVOTS = 3
BLOCKS = 8


def draw_ranks(key, part):
    draws = jax.random.randint(key, (BLOCKS, PIVOTS), 0, 20)
    levels = jnp.where(draws < 8, 1, jnp.where(draws < 15, 2, jnp.where(draws < 17, 3, jnp.where(draws < 19, 4, 6))))
    chosen = jax.random.randint(jax.random.fold_in(key, 7), (), 0, BLOCKS)
    levels = levels.at[chosen].set(6)
    return (levels * (RMAX // 6)).astype(jnp.int32)


def draw_pivots(key, part):
    middle = jax.random.permutation(jax.random.fold_in(key, 11), BLOCKS - 2)[:PIVOTS - 2].astype(jnp.int32) + 1
    ends = jnp.array([0, BLOCKS - 1], dtype=jnp.int32)
    chosen = jnp.concatenate([ends, middle])
    order = jax.random.permutation(jax.random.fold_in(key, 13), PIVOTS)
    return chosen[order].astype(jnp.int32)


def shard_levels(own_key, shape, split, least, top_value):
    def one(axis_at, parts):
        steps = jax.random.uniform(jax.random.fold_in(jax.random.fold_in(own_key, 6), axis_at), (parts,), jnp.float32, least / len(split), top_value / len(split))
        return jnp.repeat(jnp.exp(steps), shape[axis_at] // parts).reshape((-1,) + (1,) * (len(shape) - axis_at - 1))

    level = one(*split[0])
    for cut in split[1:]:
        level = level * one(*cut)
    return level


def noise(own_key, extent, width, bound, split=(), kind=jnp.bfloat16):
    factor_of = shard_levels(own_key, extent, split, -0.22, 0.18) if split else 1.0
    values = jax.random.normal(own_key, extent, jnp.float32) * width * factor_of
    return jnp.minimum(jnp.maximum(values, -bound), bound).astype(kind)


def setup_inputs(seed: int = 0, part: int = 0) -> dict:
    splits = jax.random.split(jax.random.key(seed), 7)
    own_keys = jax.random.split(jax.random.fold_in(splits[6], part), 7)
    right_side = noise(own_keys[0], (BLOCKS, BS, RHS), 1.0, 6.0, ((0, 8), (1, 2)))
    diag_inverse = noise(splits[1], (PIVOTS, BS, BS), BS ** -0.5, 0.09375, ((1, 16),))
    u_factor = noise(splits[2], (BLOCKS, PIVOTS, BS, RMAX), (RMAX // 3) ** -0.5, 0.5, ((0, 8), (2, 2)))
    v_factor = noise(splits[3], (BLOCKS, PIVOTS, BS, RMAX), BS ** -0.5, 0.09375, ((0, 8), (2, 2)))
    ranks = draw_ranks(jax.random.fold_in(splits[6], 71), part)
    pivots = draw_pivots(jax.random.fold_in(splits[6], 71), part)
    return dict(right_side=right_side, diag_inverse=diag_inverse, u_factor=u_factor, v_factor=v_factor, ranks=ranks, pivots=pivots)


def product(left, right):
    return jnp.dot(left.astype(jnp.float32), right.astype(jnp.float32), precision=lax.Precision.HIGHEST, preferred_element_type=jnp.float32)


def reference(right_side, diag_inverse, u_factor, v_factor, ranks, pivots):
    residual = right_side.astype(jnp.float32)
    columns = jnp.arange(RMAX, dtype=jnp.int32)[:, None]
    block_ids = jnp.arange(BLOCKS, dtype=jnp.int32)
    solved_list = []
    for step in range(PIVOTS):
        pivot_rhs = lax.dynamic_index_in_dim(residual, pivots[step].astype(jnp.int32), 0, keepdims=False).astype(jnp.bfloat16)
        unknowns = product(diag_inverse[step], pivot_rhs).astype(jnp.bfloat16)
        solved_list.append(unknowns)

        def per_block(item):
            v_block, u_block, rank_now = item
            coef = product(v_block.T, unknowns)
            coef = jnp.where(columns < rank_now, coef, jnp.float32(0.0)).astype(jnp.bfloat16)
            return product(u_block, coef)

        updates = lax.map(per_block, (v_factor[:, step], u_factor[:, step], ranks[:, step]))
        finished = jnp.any(block_ids[:, None] == pivots[None, :step + 1], axis=1)
        residual = residual - jnp.where(finished[:, None, None], jnp.float32(0.0), updates)
    return jnp.stack(solved_list), residual
```

```python
import functools

import jax
import jax.numpy as jnp
from jax import lax
from jax.experimental import pallas as pl
from jax.experimental.pallas import tpu as pltpu
from jax.sharding import PartitionSpec as P

PIVOTS = 3
MESH = pl.DeviceIdType.MESH


class Place:
    def __init__(self, rows):
        self.rows = rows
        self.lanes = rows // 2
        self.grp = lax.axis_index("grp")
        self.row = lax.axis_index("row")
        self.tile = lax.axis_index("tile")
        self.side = lax.rem(self.row, 2)
        self.lane = lax.div(self.row, 2)

    def peer(self, offset):
        return lax.rem(self.lane + offset, self.lanes) * 2 + self.side

    def source(self, offset):
        return lax.rem(self.lane + self.lanes - offset, self.lanes) * 2 + self.side

    def across(self, row):
        return row + 1 - 2 * self.side

    def to(self, row, tile):
        return (self.grp, row, tile)


def greet(at):
    barrier = pltpu.get_barrier_semaphore()
    targets = [at.to(at.across(at.row), at.tile), at.to(at.row, 1 - at.tile)]
    targets += [at.to(at.peer(k), at.tile) for k in range(1, at.lanes)]
    for target in targets:
        pl.semaphore_signal(barrier, inc=1, device_id=target, device_id_type=MESH)
    pl.semaphore_wait(barrier, len(targets))


def gather_body(at, src, out_at, sends, recv_col, recv_side, recv_tile):
    lanes = at.lanes
    started = []

    def send(source, slot, sem, recv, target):
        copy = pltpu.make_async_remote_copy(
            src_ref=source, dst_ref=slot, send_sem=sem, recv_sem=recv,
            device_id=target, device_id_type=MESH)
        copy.start()
        started.append(copy)

    def arrived(slot, recv):
        pltpu.make_async_remote_copy(
            src_ref=slot, dst_ref=slot, send_sem=sends.at[0], recv_sem=recv,
            device_id=at.to(at.row, 1 - at.tile), device_id_type=MESH).wait_recv()

    mine = out_at(at.row, at.tile)
    side_row = at.across(at.row)
    count = 0
    for k in range(1, lanes):
        send(src, mine, sends.at[count], recv_col.at[k], at.to(at.peer(k), at.tile))
        count += 1
    send(src, mine, sends.at[count], recv_side.at[0], at.to(side_row, at.tile))
    send(src, mine, sends.at[count + 1], recv_tile.at[0], at.to(at.row, 1 - at.tile))
    count += 2
    mine[...] = src[...]
    for k in range(1, lanes):
        slot = out_at(at.source(k), at.tile)
        arrived(slot, recv_col.at[k])
        send(slot, slot, sends.at[count], recv_side.at[k], at.to(side_row, at.tile))
        send(slot, slot, sends.at[count + 1], recv_tile.at[k], at.to(at.row, 1 - at.tile))
        count += 2
    for k in range(lanes):
        slot = out_at(at.across(at.source(k)), at.tile)
        arrived(slot, recv_side.at[k])
        send(slot, slot, sends.at[count], recv_tile.at[lanes + k], at.to(at.row, 1 - at.tile))
        count += 1
    for k in range(lanes):
        arrived(out_at(at.source(k), 1 - at.tile), recv_tile.at[k])
        arrived(out_at(at.across(at.source(k)), 1 - at.tile), recv_tile.at[lanes + k])
    for copy in started:
        copy.wait_send()


def gather_sems(rows):
    lanes = rows // 2
    return [
        pltpu.SemaphoreType.DMA((4 * lanes,)),
        pltpu.SemaphoreType.DMA((lanes,)),
        pltpu.SemaphoreType.DMA((lanes,)),
        pltpu.SemaphoreType.DMA((rows,)),
    ]


def gather_kernel(rows, src, out, sends, recv_col, recv_side, recv_tile):
    at = Place(rows)
    greet(at)
    gather_body(at, src, lambda row, tile: out.at[row, tile], sends, recv_col, recv_side, recv_tile)


def spread_kernel(rows, flags, src, out, from_side, mixed, from_col, piece,
                  sends, recv_col, recv_side, recv_tile, rs_sends, rs_side, rs_col):
    at = Place(rows)
    lanes = at.lanes
    greet(at)
    side_row = at.across(at.row)
    order = list(range(1, lanes)) + [0]
    side_copies = {}
    for k in order:
        copy = pltpu.make_async_remote_copy(
            src_ref=src.at[at.across(at.peer(k))], dst_ref=from_side.at[k],
            send_sem=rs_sends.at[k], recv_sem=rs_side.at[k],
            device_id=at.to(side_row, at.tile), device_id_type=MESH)
        copy.start()
        side_copies[k] = copy
    own = flags[0]
    col_copies = {}
    for k in order:
        side_copies[k].wait_recv()
        value = src[at.peer(k)].astype(jnp.float32) * own
        value = value + from_side[k].astype(jnp.float32) * (1.0 - own)
        mixed[k] = value.astype(jnp.bfloat16)
        if k:
            copy = pltpu.make_async_remote_copy(
                src_ref=mixed.at[k], dst_ref=from_col.at[k],
                send_sem=rs_sends.at[lanes + k], recv_sem=rs_col.at[k],
                device_id=at.to(at.peer(k), at.tile), device_id_type=MESH)
            copy.start()
            col_copies[k] = copy
    total = mixed[0].astype(jnp.float32) * flags[1]
    for k in range(1, lanes):
        col_copies[k].wait_recv()
        total = total + from_col[k].astype(jnp.float32) * flags[1 + k]
    piece[...] = total.astype(jnp.bfloat16)
    for k in order:
        side_copies[k].wait_send()
        if k:
            col_copies[k].wait_send()
    gather_body(at, piece, lambda row, tile: out.at[tile, row], sends, recv_col, recv_side, recv_tile)


def spread(rows, tiles, current, root):
    half, width = current.shape
    part = half // rows
    lanes = rows // 2
    me = lax.axis_index("row")
    lane = me // 2
    sources = lax.rem(lane + lanes - jnp.arange(lanes, dtype=jnp.int32), lanes)
    flags = jnp.concatenate([(root == me)[None], sources == root // 2]).astype(jnp.float32)
    out = pl.pallas_call(
        functools.partial(spread_kernel, rows),
        out_shape=jax.ShapeDtypeStruct((tiles, rows, part, width), jnp.bfloat16),
        in_specs=[pl.BlockSpec(memory_space=pltpu.SMEM), pl.BlockSpec(memory_space=pltpu.VMEM)],
        out_specs=pl.BlockSpec(memory_space=pltpu.VMEM),
        scratch_shapes=[
            pltpu.VMEM((lanes, part, width), jnp.bfloat16),
            pltpu.VMEM((lanes, part, width), jnp.bfloat16),
            pltpu.VMEM((lanes, part, width), jnp.bfloat16),
            pltpu.VMEM((part, width), jnp.bfloat16),
        ] + gather_sems(rows) + [
            pltpu.SemaphoreType.DMA((2 * lanes,)),
            pltpu.SemaphoreType.DMA((lanes,)),
            pltpu.SemaphoreType.DMA((lanes,)),
        ],
        compiler_params=pltpu.CompilerParams(
            collective_id=0, has_side_effects=True, vmem_limit_bytes=32 * 1024 * 1024),
        name="spread",
    )(flags, current.reshape(rows, part, width))
    return out.reshape(tiles * half, width)


def gather(rows, tiles, block):
    part, width = block.shape
    return pl.pallas_call(
        functools.partial(gather_kernel, rows),
        out_shape=jax.ShapeDtypeStruct((rows, tiles, part, width), jnp.bfloat16),
        in_specs=[pl.BlockSpec(memory_space=pltpu.VMEM)],
        out_specs=pl.BlockSpec(memory_space=pltpu.VMEM),
        scratch_shapes=gather_sems(rows),
        compiler_params=pltpu.CompilerParams(
            collective_id=1, has_side_effects=True, vmem_limit_bytes=32 * 1024 * 1024),
        name="gather",
    )(block).reshape(rows * tiles * part, width)


def local(rows, tiles, right_side, diag_inverse, u_factor, v_factor, ranks, pivots):
    residual = right_side[0].astype(jnp.float32)
    half_rows = residual.shape[0]
    rank_width = u_factor.shape[3]
    columns = lax.broadcasted_iota(jnp.int32, (rank_width, 1), 0)
    my_block = lax.axis_index("row")
    tile_at = lax.axis_index("tile")
    solved_list = []
    for step in range(PIVOTS):
        current = residual.astype(jnp.bfloat16)
        whole_pivot = spread(rows, tiles, current, pivots[step])
        part_unknowns = jnp.dot(
            diag_inverse[step], whole_pivot, preferred_element_type=jnp.float32
        ).astype(jnp.bfloat16)
        solved_list.append(part_unknowns)
        full_unknowns = gather(rows, tiles, part_unknowns)
        own_unknowns = lax.dynamic_slice_in_dim(full_unknowns, tile_at * half_rows, half_rows, 0)
        partial_value = lax.dot_general(
            v_factor[0, step],
            own_unknowns,
            (((0,), (0,)), ((), ())),
            preferred_element_type=jnp.float32,
        )
        coef = lax.psum(partial_value, "tile")
        coef = jnp.where(columns < ranks[0, step], coef, jnp.float32(0.0)).astype(jnp.bfloat16)
        update = jnp.dot(u_factor[0, step], coef, preferred_element_type=jnp.float32)
        finished = jnp.any(pivots[: step + 1] == my_block)
        residual = residual - jnp.where(finished, jnp.float32(0.0), update)
    return (jnp.stack(solved_list), residual[None])


def solution(mesh):
    in_specs = (
        P(("grp", "row"), "tile", None),
        P(None, ("row", "tile"), None),
        P("row", None, "tile", None),
        P("row", None, "tile", None),
        P("row", None),
        P(),
    )
    out_specs = (P(None, ("grp", "row", "tile"), None), P(("grp", "row"), "tile", None))
    body = functools.partial(local, mesh.shape["row"], mesh.shape["tile"])
    return jax.shard_map(body, mesh=mesh, in_specs=in_specs, out_specs=out_specs, check_vma=False)
```

```python
import functools

import jax
import jax.numpy as jnp
from jax import lax
from jax.experimental import pallas as pl
from jax.experimental.pallas import tpu as pltpu
from jax.sharding import PartitionSpec as P

PIVOTS = 3
MESH = pl.DeviceIdType.MESH


class Place:
    def __init__(self, rows):
        self.rows = rows
        self.lanes = rows // 2
        self.grp = lax.axis_index("grp")
        self.row = lax.axis_index("row")
        self.tile = lax.axis_index("tile")
        self.side = lax.rem(self.row, 2)
        self.lane = lax.div(self.row, 2)

    def peer(self, offset):
        return lax.rem(self.lane + offset, self.lanes) * 2 + self.side

    def source(self, offset):
        return lax.rem(self.lane + self.lanes - offset, self.lanes) * 2 + self.side

    def across(self, row):
        return row + 1 - 2 * self.side

    def to(self, row, tile):
        return (self.grp, row, tile)


def greet(at):
    barrier = pltpu.get_barrier_semaphore()
    targets = [at.to(at.across(at.row), at.tile), at.to(at.row, 1 - at.tile)]
    targets += [at.to(at.peer(k), at.tile) for k in range(1, at.lanes)]
    for target in targets:
        pl.semaphore_signal(barrier, inc=1, device_id=target, device_id_type=MESH)
    pl.semaphore_wait(barrier, len(targets))


def each(low, high, body):
    def step(index, carry):
        body(index)
        return carry

    lax.fori_loop(low, high, step, 0)


def gather_body(at, cuts, src, out_at, sems):
    z_right, z_left, z_recv, x_send, x_recv, t_send, t_recv = sems
    lane, last = at.lane, at.lanes - 1
    side_row = at.across(at.row)
    mate = 1 - at.tile

    def copy(source, slot, send_sem, recv_sem, target):
        return pltpu.make_async_remote_copy(
            src_ref=source, dst_ref=slot, send_sem=send_sem, recv_sem=recv_sem,
            device_id=target, device_id_type=MESH)

    def right(source, owner, cut):
        i = owner * cuts + cut
        return copy(source, out_at(owner * 2 + at.side, at.tile, cut), z_right.at[i], z_recv.at[i],
                    at.to(at.row + 2, at.tile))

    def left(source, owner, cut):
        i = owner * cuts + cut
        return copy(source, out_at(owner * 2 + at.side, at.tile, cut), z_left.at[i], z_recv.at[i],
                    at.to(at.row - 2, at.tile))

    def sidewards(source, owner, cut):
        i = owner * cuts + cut
        return copy(source, out_at(owner * 2 + at.side, at.tile, cut), x_send.at[i], x_recv.at[i],
                    at.to(side_row, at.tile))

    def to_mate(source, row, cut):
        i = row * cuts + cut
        return copy(source, out_at(row, at.tile, cut), t_send.at[i], t_recv.at[i], at.to(at.row, mate))

    def own_slot(owner, cut):
        return out_at(owner * 2 + at.side, at.tile, cut)

    def arrived(slot, sem):
        copy(slot, slot, t_send.at[0], sem, at.to(at.row, mate)).wait_recv()

    for cut in range(cuts):
        @pl.when(lane < last)
        def _(cut=cut):
            right(src.at[cut], lane, cut).start()

        @pl.when(lane > 0)
        def _(cut=cut):
            left(src.at[cut], lane, cut).start()

        sidewards(src.at[cut], lane, cut).start()
        to_mate(src.at[cut], at.row, cut).start()
    for cut in range(cuts):
        own_slot(lane, cut)[...] = src[cut]

    def from_line(owner, cut):
        slot = own_slot(owner, cut)
        arrived(slot, z_recv.at[owner * cuts + cut])
        return slot

    def from_side(owner, cut):
        row = owner * 2 + 1 - at.side
        slot = out_at(row, at.tile, cut)
        arrived(slot, x_recv.at[owner * cuts + cut])
        to_mate(slot, row, cut).start()

    def side_arrivals(k):
        for cut in range(cuts):
            @pl.when(lane >= k)
            def _(cut=cut):
                from_side(lane - k, cut)

            @pl.when(jnp.logical_and(lane + k <= last, k > 0))
            def _(cut=cut):
                from_side(lane + k, cut)

    def hop(k):
        for cut in range(cuts):
            @pl.when(lane >= k)
            def _(cut=cut):
                slot = from_line(lane - k, cut)

                @pl.when(lane < last)
                def _():
                    right(slot, lane - k, cut).start()

                sidewards(slot, lane - k, cut).start()
                to_mate(slot, (lane - k) * 2 + at.side, cut).start()

            @pl.when(lane + k <= last)
            def _(cut=cut):
                slot = from_line(lane + k, cut)

                @pl.when(lane > 0)
                def _():
                    left(slot, lane + k, cut).start()

                sidewards(slot, lane + k, cut).start()
                to_mate(slot, (lane + k) * 2 + at.side, cut).start()
        side_arrivals(k - 1)

    each(1, at.lanes, hop)
    side_arrivals(last)

    def finish(owner):
        for cut in range(cuts):
            slot = own_slot(owner, cut)

            @pl.when(jnp.logical_and(owner <= lane, lane < last))
            def _(slot=slot, cut=cut):
                right(slot, owner, cut).wait_send()

            @pl.when(jnp.logical_and(owner >= lane, lane > 0))
            def _(slot=slot, cut=cut):
                left(slot, owner, cut).wait_send()

            sidewards(slot, owner, cut).wait_send()
            for side in range(2):
                row = owner * 2 + side
                arrived(out_at(row, mate, cut), t_recv.at[row * cuts + cut])
                to_mate(out_at(row, at.tile, cut), row, cut).wait_send()

    each(0, at.lanes, finish)


def cuts_of(part):
    return max(1, min(4, part // 16))


def gather_sems(rows, cuts):
    column = pltpu.SemaphoreType.DMA((rows // 2 * cuts,))
    whole = pltpu.SemaphoreType.DMA((rows * cuts,))
    return [column] * 5 + [whole] * 2


def gather_kernel(rows, cuts, src, out, *sems):
    at = Place(rows)
    greet(at)
    gather_body(at, cuts, src, lambda row, tile, cut: out.at[row, tile, cut], sems)


def spread_kernel(rows, cuts, flags, src, out, from_side, mixed, from_col, piece,
                  rs_sends, rs_side, rs_col, *sems):
    at = Place(rows)
    lanes = at.lanes
    greet(at)
    side_row = at.across(at.row)
    order = list(range(1, lanes)) + [0]
    side_copies = {}
    for k in order:
        copy = pltpu.make_async_remote_copy(
            src_ref=src.at[at.across(at.peer(k))], dst_ref=from_side.at[k],
            send_sem=rs_sends.at[k], recv_sem=rs_side.at[k],
            device_id=at.to(side_row, at.tile), device_id_type=MESH)
        copy.start()
        side_copies[k] = copy
    own = flags[0]
    col_copies = {}
    for k in order:
        side_copies[k].wait_recv()
        value = src[at.peer(k)].astype(jnp.float32) * own
        value = value + from_side[k].astype(jnp.float32) * (1.0 - own)
        mixed[k] = value.astype(jnp.bfloat16)
        if k:
            copy = pltpu.make_async_remote_copy(
                src_ref=mixed.at[k], dst_ref=from_col.at[k],
                send_sem=rs_sends.at[lanes + k], recv_sem=rs_col.at[k],
                device_id=at.to(at.peer(k), at.tile), device_id_type=MESH)
            copy.start()
            col_copies[k] = copy
    total = mixed[0].astype(jnp.float32) * flags[1]
    for k in range(1, lanes):
        col_copies[k].wait_recv()
        total = total + from_col[k].astype(jnp.float32) * flags[1 + k]
    piece[...] = total.astype(jnp.bfloat16).reshape(piece.shape)
    for k in order:
        side_copies[k].wait_send()
        if k:
            col_copies[k].wait_send()
    gather_body(at, cuts, piece, lambda row, tile, cut: out.at[tile, row, cut], sems)


def spread(rows, tiles, current, root):
    half, width = current.shape
    part = half // rows
    lanes = rows // 2
    cuts = cuts_of(part)
    me = lax.axis_index("row")
    lane = me // 2
    sources = lax.rem(lane + lanes - jnp.arange(lanes, dtype=jnp.int32), lanes)
    flags = jnp.concatenate([(root == me)[None], sources == root // 2]).astype(jnp.float32)
    out = pl.pallas_call(
        functools.partial(spread_kernel, rows, cuts),
        out_shape=jax.ShapeDtypeStruct((tiles, rows, cuts, part // cuts, width), jnp.bfloat16),
        in_specs=[pl.BlockSpec(memory_space=pltpu.SMEM), pl.BlockSpec(memory_space=pltpu.VMEM)],
        out_specs=pl.BlockSpec(memory_space=pltpu.VMEM),
        scratch_shapes=[
            pltpu.VMEM((lanes, part, width), jnp.bfloat16),
            pltpu.VMEM((lanes, part, width), jnp.bfloat16),
            pltpu.VMEM((lanes, part, width), jnp.bfloat16),
            pltpu.VMEM((cuts, part // cuts, width), jnp.bfloat16),
            pltpu.SemaphoreType.DMA((2 * lanes,)),
            pltpu.SemaphoreType.DMA((lanes,)),
            pltpu.SemaphoreType.DMA((lanes,)),
        ] + gather_sems(rows, cuts),
        compiler_params=pltpu.CompilerParams(
            collective_id=0, has_side_effects=True, vmem_limit_bytes=32 * 1024 * 1024),
        name="spread",
    )(flags, current.reshape(rows, part, width))
    return out.reshape(tiles * half, width)


def gather(rows, tiles, block):
    part, width = block.shape
    cuts = cuts_of(part)
    return pl.pallas_call(
        functools.partial(gather_kernel, rows, cuts),
        out_shape=jax.ShapeDtypeStruct((rows, tiles, cuts, part // cuts, width), jnp.bfloat16),
        in_specs=[pl.BlockSpec(memory_space=pltpu.VMEM)],
        out_specs=pl.BlockSpec(memory_space=pltpu.VMEM),
        scratch_shapes=gather_sems(rows, cuts),
        compiler_params=pltpu.CompilerParams(
            collective_id=1, has_side_effects=True, vmem_limit_bytes=32 * 1024 * 1024),
        name="gather",
    )(block.reshape(cuts, part // cuts, width)).reshape(rows * tiles * part, width)


def local(rows, tiles, right_side, diag_inverse, u_factor, v_factor, ranks, pivots):
    residual = right_side[0].astype(jnp.float32)
    half_rows = residual.shape[0]
    rank_width = u_factor.shape[3]
    columns = lax.broadcasted_iota(jnp.int32, (rank_width, 1), 0)
    my_block = lax.axis_index("row")
    tile_at = lax.axis_index("tile")
    solved_list = []
    for step in range(PIVOTS):
        current = residual.astype(jnp.bfloat16)
        whole_pivot = spread(rows, tiles, current, pivots[step])
        part_unknowns = jnp.dot(
            diag_inverse[step], whole_pivot, preferred_element_type=jnp.float32
        ).astype(jnp.bfloat16)
        solved_list.append(part_unknowns)
        full_unknowns = gather(rows, tiles, part_unknowns)
        own_unknowns = lax.dynamic_slice_in_dim(full_unknowns, tile_at * half_rows, half_rows, 0)
        partial_value = lax.dot_general(
            v_factor[0, step],
            own_unknowns,
            (((0,), (0,)), ((), ())),
            preferred_element_type=jnp.float32,
        )
        coef = lax.psum(partial_value, "tile")
        coef = jnp.where(columns < ranks[0, step], coef, jnp.float32(0.0)).astype(jnp.bfloat16)
        update = jnp.dot(u_factor[0, step], coef, preferred_element_type=jnp.float32)
        finished = jnp.any(pivots[: step + 1] == my_block)
        residual = residual - jnp.where(finished, jnp.float32(0.0), update)
    return (jnp.stack(solved_list), residual[None])


def solution(mesh):
    in_specs = (
        P(("grp", "row"), "tile", None),
        P(None, ("row", "tile"), None),
        P("row", None, "tile", None),
        P("row", None, "tile", None),
        P("row", None),
        P(),
    )
    out_specs = (P(None, ("grp", "row", "tile"), None), P(("grp", "row"), "tile", None))
    body = functools.partial(local, mesh.shape["row"], mesh.shape["tile"])
    return jax.shard_map(body, mesh=mesh, in_specs=in_specs, out_specs=out_specs, check_vma=False)
```

```python
import functools

import jax
import jax.numpy as jnp
from jax import lax
from jax.experimental import pallas as pl
from jax.experimental.pallas import tpu as pltpu
from jax.sharding import PartitionSpec as P

PIVOTS = 3
MESH = pl.DeviceIdType.MESH


class Place:
    def __init__(self, rows):
        self.rows = rows
        self.lanes = rows // 2
        self.grp = lax.axis_index("grp")
        self.row = lax.axis_index("row")
        self.tile = lax.axis_index("tile")
        self.side = lax.rem(self.row, 2)
        self.lane = lax.div(self.row, 2)

    def peer(self, offset):
        return lax.rem(self.lane + offset, self.lanes) * 2 + self.side

    def source(self, offset):
        return lax.rem(self.lane + self.lanes - offset, self.lanes) * 2 + self.side

    def across(self, row):
        return row + 1 - 2 * self.side

    def to(self, row, tile):
        return (self.grp, row, tile)


def greet(at):
    barrier = pltpu.get_barrier_semaphore()
    targets = [at.to(at.across(at.row), at.tile), at.to(at.row, 1 - at.tile)]
    targets += [at.to(at.peer(k), at.tile) for k in range(1, at.lanes)]
    for target in targets:
        pl.semaphore_signal(barrier, inc=1, device_id=target, device_id_type=MESH)
    pl.semaphore_wait(barrier, len(targets))


def each(low, high, body):
    def step(index, carry):
        body(index)
        return carry

    lax.fori_loop(low, high, step, 0)


def gather_body(at, cuts, src, out_at, sems):
    z_right, z_left, z_recv, x_send, x_recv, t_send, t_recv = sems
    lane, last = at.lane, at.lanes - 1
    side_row = at.across(at.row)
    mate = 1 - at.tile

    def copy(source, slot, send_sem, recv_sem, target):
        return pltpu.make_async_remote_copy(
            src_ref=source, dst_ref=slot, send_sem=send_sem, recv_sem=recv_sem,
            device_id=target, device_id_type=MESH)

    def right(source, owner, cut):
        i = owner * cuts + cut
        return copy(source, out_at(owner * 2 + at.side, at.tile, cut), z_right.at[i], z_recv.at[i],
                    at.to(at.row + 2, at.tile))

    def left(source, owner, cut):
        i = owner * cuts + cut
        return copy(source, out_at(owner * 2 + at.side, at.tile, cut), z_left.at[i], z_recv.at[i],
                    at.to(at.row - 2, at.tile))

    def sidewards(source, owner, cut):
        i = owner * cuts + cut
        return copy(source, out_at(owner * 2 + at.side, at.tile, cut), x_send.at[i], x_recv.at[i],
                    at.to(side_row, at.tile))

    def to_mate(source, row, cut):
        i = row * cuts + cut
        return copy(source, out_at(row, at.tile, cut), t_send.at[i], t_recv.at[i], at.to(at.row, mate))

    def own_slot(owner, cut):
        return out_at(owner * 2 + at.side, at.tile, cut)

    def arrived(slot, sem):
        copy(slot, slot, t_send.at[0], sem, at.to(at.row, mate)).wait_recv()

    for cut in range(cuts):
        @pl.when(lane < last)
        def _(cut=cut):
            right(src.at[cut], lane, cut).start()

        @pl.when(lane > 0)
        def _(cut=cut):
            left(src.at[cut], lane, cut).start()

        sidewards(src.at[cut], lane, cut).start()
        to_mate(src.at[cut], at.row, cut).start()
    for cut in range(cuts):
        own_slot(lane, cut)[...] = src[cut]

    def from_line(owner, cut):
        slot = own_slot(owner, cut)
        arrived(slot, z_recv.at[owner * cuts + cut])
        return slot

    def from_side(owner, cut):
        row = owner * 2 + 1 - at.side
        slot = out_at(row, at.tile, cut)
        arrived(slot, x_recv.at[owner * cuts + cut])
        to_mate(slot, row, cut).start()

    def side_arrivals(k):
        for cut in range(cuts):
            @pl.when(lane >= k)
            def _(cut=cut):
                from_side(lane - k, cut)

            @pl.when(jnp.logical_and(lane + k <= last, k > 0))
            def _(cut=cut):
                from_side(lane + k, cut)

    def hop(k):
        for cut in range(cuts):
            @pl.when(lane >= k)
            def _(cut=cut):
                slot = from_line(lane - k, cut)

                @pl.when(lane < last)
                def _():
                    right(slot, lane - k, cut).start()

                sidewards(slot, lane - k, cut).start()
                to_mate(slot, (lane - k) * 2 + at.side, cut).start()

            @pl.when(lane + k <= last)
            def _(cut=cut):
                slot = from_line(lane + k, cut)

                @pl.when(lane > 0)
                def _():
                    left(slot, lane + k, cut).start()

                sidewards(slot, lane + k, cut).start()
                to_mate(slot, (lane + k) * 2 + at.side, cut).start()
        side_arrivals(k - 1)

    each(1, at.lanes, hop)
    side_arrivals(last)

    def finish(owner):
        for cut in range(cuts):
            slot = own_slot(owner, cut)

            @pl.when(jnp.logical_and(owner <= lane, lane < last))
            def _(slot=slot, cut=cut):
                right(slot, owner, cut).wait_send()

            @pl.when(jnp.logical_and(owner >= lane, lane > 0))
            def _(slot=slot, cut=cut):
                left(slot, owner, cut).wait_send()

            sidewards(slot, owner, cut).wait_send()
            for side in range(2):
                row = owner * 2 + side
                arrived(out_at(row, mate, cut), t_recv.at[row * cuts + cut])
                to_mate(out_at(row, at.tile, cut), row, cut).wait_send()

    each(0, at.lanes, finish)


def cuts_of(part):
    return max(1, min(4, part // 16))


def gather_sems(rows, cuts):
    column = pltpu.SemaphoreType.DMA((rows // 2 * cuts,))
    whole = pltpu.SemaphoreType.DMA((rows * cuts,))
    return [column] * 5 + [whole] * 2


def indicator(condition):
    return jnp.where(condition, jnp.float32(1.0), jnp.float32(0.0))


def solve_kernel(rows, cuts, step, pivots, ranks, pivot_block, diag, u_hbm, v_hbm, residual,
                 solved, new_residual, current, diag_buf, u_buf, v_buf, res_buf, total, piece, full,
                 partial, other, load_sems, mate_send, mate_recv, *sems):
    at = Place(rows)
    part, width = solved.shape
    loads = [
        pltpu.make_async_copy(diag.at[step], diag_buf, load_sems.at[0]),
        pltpu.make_async_copy(v_hbm.at[0, step], v_buf, load_sems.at[1]),
        pltpu.make_async_copy(u_hbm.at[0, step], u_buf, load_sems.at[2]),
        pltpu.make_async_copy(residual, res_buf, load_sems.at[3]),
    ]
    for load in loads:
        load.start()
    greet(at)
    loads[0].wait()
    depth = diag_buf.shape[1]
    span = depth // 8
    total[...] = jnp.zeros_like(total)

    def product(i):
        k = pl.multiple_of(i * span, span)
        total[...] += jnp.dot(diag_buf[:, pl.ds(k, span)], pivot_block[pl.ds(k, span), :],
                              preferred_element_type=jnp.float32)

    each(0, 8, product)
    own = total[...].astype(jnp.bfloat16)
    solved[...] = own
    piece[...] = own.reshape(piece.shape)
    gather_body(at, cuts, piece, lambda row, tile, cut: full.at[row, tile, cut], sems)
    loads[1].wait()
    partial[...] = jnp.zeros_like(partial)
    lanes = at.lanes

    def inner(i):
        k = pl.multiple_of(i * part, part)
        values = full[at.tile * lanes + lax.div(i, 2), lax.rem(i, 2)].reshape(part, width)
        partial[...] += lax.dot_general(v_buf[pl.ds(k, part), :], values, (((0,), (0,)), ((), ())),
                                        preferred_element_type=jnp.float32)

    each(0, rows, inner)
    swap = pltpu.make_async_remote_copy(
        src_ref=partial, dst_ref=other, send_sem=mate_send, recv_sem=mate_recv,
        device_id=at.to(at.row, 1 - at.tile), device_id_type=MESH)
    swap.start()
    loads[2].wait()
    loads[3].wait()
    swap.wait()
    columns = lax.broadcasted_iota(jnp.int32, partial.shape, 0)
    coef = jnp.where(columns < ranks[0, step], partial[...] + other[...], jnp.float32(0.0))
    coef = coef.astype(jnp.bfloat16)
    keep = jnp.float32(1.0)
    for p in range(step + 1):
        keep = keep * indicator(pivots[p] != at.row)
    height = res_buf.shape[0]
    block = height // 8

    def outer(i):
        k = pl.ds(pl.multiple_of(i * block, block), block)
        update = jnp.dot(u_buf[k, :], coef, preferred_element_type=jnp.float32)
        value = res_buf[k, :] - update * keep
        new_residual[k, :] = value
        current[k, :] = value.astype(jnp.bfloat16)

    each(0, 8, outer)


def spread_kernel(rows, cuts, step, pivots, src, out, from_side, mixed, from_col, piece,
                  rs_sends, rs_side, rs_col, *sems):
    at = Place(rows)
    lanes = at.lanes
    greet(at)
    side_row = at.across(at.row)
    order = list(range(1, lanes)) + [0]
    side_copies = {}
    for k in order:
        copy = pltpu.make_async_remote_copy(
            src_ref=src.at[at.across(at.peer(k))], dst_ref=from_side.at[k],
            send_sem=rs_sends.at[k], recv_sem=rs_side.at[k],
            device_id=at.to(side_row, at.tile), device_id_type=MESH)
        copy.start()
        side_copies[k] = copy
    root = pivots[step]
    own = indicator(root == at.row)
    root_lane = lax.div(root, 2)
    col_copies = {}
    for k in order:
        side_copies[k].wait_recv()
        value = src[at.peer(k)].astype(jnp.float32) * own
        value = value + from_side[k].astype(jnp.float32) * (1.0 - own)
        mixed[k] = value.astype(jnp.bfloat16)
        if k:
            copy = pltpu.make_async_remote_copy(
                src_ref=mixed.at[k], dst_ref=from_col.at[k],
                send_sem=rs_sends.at[lanes + k], recv_sem=rs_col.at[k],
                device_id=at.to(at.peer(k), at.tile), device_id_type=MESH)
            copy.start()
            col_copies[k] = copy
    total = mixed[0].astype(jnp.float32) * indicator(root_lane == at.lane)
    for k in range(1, lanes):
        col_copies[k].wait_recv()
        total = total + from_col[k].astype(jnp.float32) * indicator(root_lane == lax.div(at.source(k), 2))
    piece[...] = total.astype(jnp.bfloat16).reshape(piece.shape)
    for k in order:
        side_copies[k].wait_send()
        if k:
            col_copies[k].wait_send()
    gather_body(at, cuts, piece, lambda row, tile, cut: out.at[tile, row, cut], sems)


def spread(rows, tiles, step, current, pivots):
    half, width = current.shape
    part = half // rows
    lanes = rows // 2
    cuts = cuts_of(part)
    out = pl.pallas_call(
        functools.partial(spread_kernel, rows, cuts, step),
        out_shape=jax.ShapeDtypeStruct((tiles, rows, cuts, part // cuts, width), jnp.bfloat16),
        in_specs=[pl.BlockSpec(memory_space=pltpu.SMEM), pl.BlockSpec(memory_space=pltpu.VMEM)],
        out_specs=pl.BlockSpec(memory_space=pltpu.VMEM),
        scratch_shapes=[
            pltpu.VMEM((lanes, part, width), jnp.bfloat16),
            pltpu.VMEM((lanes, part, width), jnp.bfloat16),
            pltpu.VMEM((lanes, part, width), jnp.bfloat16),
            pltpu.VMEM((cuts, part // cuts, width), jnp.bfloat16),
            pltpu.SemaphoreType.DMA((2 * lanes,)),
            pltpu.SemaphoreType.DMA((lanes,)),
            pltpu.SemaphoreType.DMA((lanes,)),
        ] + gather_sems(rows, cuts),
        compiler_params=pltpu.CompilerParams(
            collective_id=2 * step, has_side_effects=True, vmem_limit_bytes=32 * 1024 * 1024),
        name="spread",
    )(pivots, current.reshape(rows, part, width))
    return out.reshape(tiles * half, width)


def solve(rows, tiles, step, pivots, ranks, pivot_block, diag, u_factor, v_factor, residual):
    part, depth = diag.shape[1:]
    height, width = residual.shape
    rank_width = u_factor.shape[3]
    cuts = cuts_of(part)
    smem = pl.BlockSpec(memory_space=pltpu.SMEM)
    vmem = pl.BlockSpec(memory_space=pltpu.VMEM)
    anywhere = pl.BlockSpec(memory_space=pl.ANY)
    return pl.pallas_call(
        functools.partial(solve_kernel, rows, cuts, step),
        out_shape=(
            jax.ShapeDtypeStruct((part, width), jnp.bfloat16),
            jax.ShapeDtypeStruct((height, width), jnp.float32),
            jax.ShapeDtypeStruct((height, width), jnp.bfloat16),
        ),
        in_specs=[smem, smem, vmem, anywhere, anywhere, anywhere, anywhere],
        out_specs=(vmem, vmem, vmem),
        scratch_shapes=[
            pltpu.VMEM((part, depth), jnp.bfloat16),
            pltpu.VMEM((height, rank_width), jnp.bfloat16),
            pltpu.VMEM((height, rank_width), jnp.bfloat16),
            pltpu.VMEM((height, width), jnp.float32),
            pltpu.VMEM((part, width), jnp.float32),
            pltpu.VMEM((cuts, part // cuts, width), jnp.bfloat16),
            pltpu.VMEM((rows, tiles, cuts, part // cuts, width), jnp.bfloat16),
            pltpu.VMEM((rank_width, width), jnp.float32),
            pltpu.VMEM((rank_width, width), jnp.float32),
            pltpu.SemaphoreType.DMA((4,)),
            pltpu.SemaphoreType.DMA,
            pltpu.SemaphoreType.DMA,
        ] + gather_sems(rows, cuts),
        compiler_params=pltpu.CompilerParams(
            collective_id=2 * step + 1, has_side_effects=True, vmem_limit_bytes=40 * 1024 * 1024),
        name="solve",
    )(pivots, ranks, pivot_block, diag, u_factor, v_factor, residual)


def local(rows, tiles, right_side, diag_inverse, u_factor, v_factor, ranks, pivots):
    current = right_side[0]
    residual = current.astype(jnp.float32)
    solved_list = []
    for step in range(PIVOTS):
        pivot_block = spread(rows, tiles, step, current, pivots)
        solved, residual, current = solve(
            rows, tiles, step, pivots, ranks, pivot_block, diag_inverse, u_factor, v_factor, residual)
        solved_list.append(solved)
    return (jnp.stack(solved_list), residual[None])


def solution(mesh):
    in_specs = (
        P(("grp", "row"), "tile", None),
        P(None, ("row", "tile"), None),
        P("row", None, "tile", None),
        P("row", None, "tile", None),
        P("row", None),
        P(),
    )
    out_specs = (P(None, ("grp", "row", "tile"), None), P(("grp", "row"), "tile", None))
    body = functools.partial(local, mesh.shape["row"], mesh.shape["tile"])
    return jax.shard_map(body, mesh=mesh, in_specs=in_specs, out_specs=out_specs, check_vma=False)
```

```python
import functools

import jax
import jax.numpy as jnp
from jax import lax
from jax.experimental import pallas as pl
from jax.experimental.pallas import tpu as pltpu
from jax.sharding import PartitionSpec as P

PIVOTS = 3
MESH = pl.DeviceIdType.MESH


class Place:
    def __init__(self, rows):
        self.rows = rows
        self.lanes = rows // 2
        self.grp = lax.axis_index("grp")
        self.row = lax.axis_index("row")
        self.tile = lax.axis_index("tile")
        self.side = lax.rem(self.row, 2)
        self.lane = lax.div(self.row, 2)

    def peer(self, offset):
        return lax.rem(self.lane + offset, self.lanes) * 2 + self.side

    def source(self, offset):
        return lax.rem(self.lane + self.lanes - offset, self.lanes) * 2 + self.side

    def across(self, row):
        return row + 1 - 2 * self.side

    def to(self, row, tile):
        return (self.grp, row, tile)


def greet(at):
    barrier = pltpu.get_barrier_semaphore()
    targets = [at.to(at.across(at.row), at.tile), at.to(at.row, 1 - at.tile)]
    targets += [at.to(at.peer(k), at.tile) for k in range(1, at.lanes)]
    for target in targets:
        pl.semaphore_signal(barrier, inc=1, device_id=target, device_id_type=MESH)
    pl.semaphore_wait(barrier, len(targets))


def each(low, high, body):
    def step(index, carry):
        body(index)
        return carry

    lax.fori_loop(low, high, step, 0)


def gather_body(at, cuts, src, out_at, sems, ready=None):
    z_right, z_left, z_recv, x_send, x_recv, t_send, t_recv = sems
    lane, last = at.lane, at.lanes - 1
    side_row = at.across(at.row)
    mate = 1 - at.tile

    def copy(source, slot, send_sem, recv_sem, target):
        return pltpu.make_async_remote_copy(
            src_ref=source, dst_ref=slot, send_sem=send_sem, recv_sem=recv_sem,
            device_id=target, device_id_type=MESH)

    def right(source, owner, cut):
        i = owner * cuts + cut
        return copy(source, out_at(owner * 2 + at.side, at.tile, cut), z_right.at[i], z_recv.at[i],
                    at.to(at.row + 2, at.tile))

    def left(source, owner, cut):
        i = owner * cuts + cut
        return copy(source, out_at(owner * 2 + at.side, at.tile, cut), z_left.at[i], z_recv.at[i],
                    at.to(at.row - 2, at.tile))

    def sidewards(source, owner, cut):
        i = owner * cuts + cut
        return copy(source, out_at(owner * 2 + at.side, at.tile, cut), x_send.at[i], x_recv.at[i],
                    at.to(side_row, at.tile))

    def to_mate(source, row, cut):
        i = row * cuts + cut
        return copy(source, out_at(row, at.tile, cut), t_send.at[i], t_recv.at[i], at.to(at.row, mate))

    def own_slot(owner, cut):
        return out_at(owner * 2 + at.side, at.tile, cut)

    def arrived(slot, sem):
        copy(slot, slot, t_send.at[0], sem, at.to(at.row, mate)).wait_recv()

    for cut in range(cuts):
        if ready is not None:
            ready(cut)

        @pl.when(lane < last)
        def _(cut=cut):
            right(src.at[cut], lane, cut).start()

        @pl.when(lane > 0)
        def _(cut=cut):
            left(src.at[cut], lane, cut).start()

        sidewards(src.at[cut], lane, cut).start()
        to_mate(src.at[cut], at.row, cut).start()
    for cut in range(cuts):
        own_slot(lane, cut)[...] = src[cut]

    def from_line(owner, cut):
        slot = own_slot(owner, cut)
        arrived(slot, z_recv.at[owner * cuts + cut])
        return slot

    def from_side(owner, cut):
        row = owner * 2 + 1 - at.side
        slot = out_at(row, at.tile, cut)
        arrived(slot, x_recv.at[owner * cuts + cut])
        to_mate(slot, row, cut).start()

    def side_arrivals(k):
        for cut in range(cuts):
            @pl.when(lane >= k)
            def _(cut=cut):
                from_side(lane - k, cut)

            @pl.when(jnp.logical_and(lane + k <= last, k > 0))
            def _(cut=cut):
                from_side(lane + k, cut)

    def hop(k):
        for cut in range(cuts):
            @pl.when(lane >= k)
            def _(cut=cut):
                slot = from_line(lane - k, cut)

                @pl.when(lane < last)
                def _():
                    right(slot, lane - k, cut).start()

                sidewards(slot, lane - k, cut).start()
                to_mate(slot, (lane - k) * 2 + at.side, cut).start()

            @pl.when(lane + k <= last)
            def _(cut=cut):
                slot = from_line(lane + k, cut)

                @pl.when(lane > 0)
                def _():
                    left(slot, lane + k, cut).start()

                sidewards(slot, lane + k, cut).start()
                to_mate(slot, (lane + k) * 2 + at.side, cut).start()
        side_arrivals(k - 1)

    each(1, at.lanes, hop)
    side_arrivals(last)

    def finish(owner):
        for cut in range(cuts):
            slot = own_slot(owner, cut)

            @pl.when(jnp.logical_and(owner <= lane, lane < last))
            def _(slot=slot, cut=cut):
                right(slot, owner, cut).wait_send()

            @pl.when(jnp.logical_and(owner >= lane, lane > 0))
            def _(slot=slot, cut=cut):
                left(slot, owner, cut).wait_send()

            sidewards(slot, owner, cut).wait_send()
            for side in range(2):
                row = owner * 2 + side
                arrived(out_at(row, mate, cut), t_recv.at[row * cuts + cut])
                to_mate(out_at(row, at.tile, cut), row, cut).wait_send()

    each(0, at.lanes, finish)


def cuts_of(part):
    return max(1, min(4, part // 16))


def gather_sems(rows, cuts):
    column = pltpu.SemaphoreType.DMA((rows // 2 * cuts,))
    whole = pltpu.SemaphoreType.DMA((rows * cuts,))
    return [column] * 5 + [whole] * 2


def indicator(condition):
    return jnp.where(condition, jnp.float32(1.0), jnp.float32(0.0))


def solve_kernel(rows, cuts, step, pivots, ranks, pivot_block, diag, u_hbm, v_hbm, residual,
                 solved, new_residual, current, diag_buf, u_buf, v_buf, res_buf, total, piece, full,
                 partial, other, load_sems, mate_send, mate_recv, *sems):
    at = Place(rows)
    part, width = solved.shape
    loads = [
        pltpu.make_async_copy(diag.at[step], diag_buf, load_sems.at[0]),
        pltpu.make_async_copy(v_hbm.at[0, step], v_buf, load_sems.at[1]),
        pltpu.make_async_copy(u_hbm.at[0, step], u_buf, load_sems.at[2]),
        pltpu.make_async_copy(residual, res_buf, load_sems.at[3]),
    ]
    for load in loads:
        load.start()
    greet(at)
    loads[0].wait()
    depth = diag_buf.shape[1]
    span = depth // 8
    total[...] = jnp.zeros_like(total)

    def product(i):
        k = pl.multiple_of(i * span, span)
        total[...] += jnp.dot(diag_buf[:, pl.ds(k, span)], pivot_block[pl.ds(k, span), :],
                              preferred_element_type=jnp.float32)

    each(0, 8, product)
    own = total[...].astype(jnp.bfloat16)
    solved[...] = own
    piece[...] = own.reshape(piece.shape)
    gather_body(at, cuts, piece, lambda row, tile, cut: full.at[row, tile, cut], sems)
    loads[1].wait()
    partial[...] = jnp.zeros_like(partial)
    lanes = at.lanes

    def inner(i):
        k = pl.multiple_of(i * part, part)
        values = full[at.tile * lanes + lax.div(i, 2), lax.rem(i, 2)].reshape(part, width)
        partial[...] += lax.dot_general(v_buf[pl.ds(k, part), :], values, (((0,), (0,)), ((), ())),
                                        preferred_element_type=jnp.float32)

    each(0, rows, inner)
    swap = pltpu.make_async_remote_copy(
        src_ref=partial, dst_ref=other, send_sem=mate_send, recv_sem=mate_recv,
        device_id=at.to(at.row, 1 - at.tile), device_id_type=MESH)
    swap.start()
    loads[2].wait()
    loads[3].wait()
    swap.wait()
    columns = lax.broadcasted_iota(jnp.int32, partial.shape, 0)
    coef = jnp.where(columns < ranks[0, step], partial[...] + other[...], jnp.float32(0.0))
    coef = coef.astype(jnp.bfloat16)
    keep = jnp.float32(1.0)
    for p in range(step + 1):
        keep = keep * indicator(pivots[p] != at.row)
    height = res_buf.shape[0]
    block = height // 8

    def outer(i):
        k = pl.ds(pl.multiple_of(i * block, block), block)
        update = jnp.dot(u_buf[k, :], coef, preferred_element_type=jnp.float32)
        value = res_buf[k, :] - update * keep
        new_residual[k, :] = value
        current[k, :] = value.astype(jnp.bfloat16)

    each(0, 8, outer)


def spread_kernel(rows, cuts, step, pivots, src, out, from_side, mixed, from_col, piece,
                  rs_sends, rs_side, rs_col, *sems):
    at = Place(rows)
    lanes = at.lanes
    greet(at)
    side_row = at.across(at.row)
    order = list(range(1, lanes)) + [0]
    side_copies = {}
    for cut in range(cuts):
        for k in order:
            i = cut * lanes + k
            copy = pltpu.make_async_remote_copy(
                src_ref=src.at[at.across(at.peer(k)), cut], dst_ref=from_side.at[i],
                send_sem=rs_sends.at[i], recv_sem=rs_side.at[i],
                device_id=at.to(side_row, at.tile), device_id_type=MESH)
            copy.start()
            side_copies[i] = copy
    root = pivots[step]
    own = indicator(root == at.row)
    root_lane = lax.div(root, 2)
    col_copies = {}

    def mix(cut):
        for k in order:
            i = cut * lanes + k
            side_copies[i].wait_recv()
            value = src[at.peer(k), cut].astype(jnp.float32) * own
            value = value + from_side[i].astype(jnp.float32) * (1.0 - own)
            mixed[i] = value.astype(jnp.bfloat16)
            if k:
                copy = pltpu.make_async_remote_copy(
                    src_ref=mixed.at[i], dst_ref=from_col.at[i],
                    send_sem=rs_sends.at[cuts * lanes + i], recv_sem=rs_col.at[i],
                    device_id=at.to(at.peer(k), at.tile), device_id_type=MESH)
                copy.start()
                col_copies[i] = copy

    def ready(cut):
        if cut == 0:
            mix(0)
        if cut + 1 < cuts:
            mix(cut + 1)
        total = mixed[cut * lanes].astype(jnp.float32) * indicator(root_lane == at.lane)
        for k in range(1, lanes):
            i = cut * lanes + k
            col_copies[i].wait_recv()
            total = total + from_col[i].astype(jnp.float32) * indicator(
                root_lane == lax.div(at.source(k), 2))
        piece[cut] = total.astype(jnp.bfloat16)

    gather_body(at, cuts, piece, lambda row, tile, cut: out.at[tile, row, cut], sems, ready)
    for copy in list(side_copies.values()) + list(col_copies.values()):
        copy.wait_send()


def spread(rows, tiles, step, current, pivots):
    half, width = current.shape
    part = half // rows
    lanes = rows // 2
    cuts = cuts_of(part)
    out = pl.pallas_call(
        functools.partial(spread_kernel, rows, cuts, step),
        out_shape=jax.ShapeDtypeStruct((tiles, rows, cuts, part // cuts, width), jnp.bfloat16),
        in_specs=[pl.BlockSpec(memory_space=pltpu.SMEM), pl.BlockSpec(memory_space=pltpu.VMEM)],
        out_specs=pl.BlockSpec(memory_space=pltpu.VMEM),
        scratch_shapes=[
            pltpu.VMEM((cuts * lanes, part // cuts, width), jnp.bfloat16),
            pltpu.VMEM((cuts * lanes, part // cuts, width), jnp.bfloat16),
            pltpu.VMEM((cuts * lanes, part // cuts, width), jnp.bfloat16),
            pltpu.VMEM((cuts, part // cuts, width), jnp.bfloat16),
            pltpu.SemaphoreType.DMA((2 * cuts * lanes,)),
            pltpu.SemaphoreType.DMA((cuts * lanes,)),
            pltpu.SemaphoreType.DMA((cuts * lanes,)),
        ] + gather_sems(rows, cuts),
        compiler_params=pltpu.CompilerParams(
            collective_id=2 * step, has_side_effects=True, vmem_limit_bytes=32 * 1024 * 1024),
        name="spread",
    )(pivots, current.reshape(rows, cuts, part // cuts, width))
    return out.reshape(tiles * half, width)


def solve(rows, tiles, step, pivots, ranks, pivot_block, diag, u_factor, v_factor, residual):
    part, depth = diag.shape[1:]
    height, width = residual.shape
    rank_width = u_factor.shape[3]
    cuts = cuts_of(part)
    smem = pl.BlockSpec(memory_space=pltpu.SMEM)
    vmem = pl.BlockSpec(memory_space=pltpu.VMEM)
    anywhere = pl.BlockSpec(memory_space=pl.ANY)
    return pl.pallas_call(
        functools.partial(solve_kernel, rows, cuts, step),
        out_shape=(
            jax.ShapeDtypeStruct((part, width), jnp.bfloat16),
            jax.ShapeDtypeStruct((height, width), jnp.float32),
            jax.ShapeDtypeStruct((height, width), jnp.bfloat16),
        ),
        in_specs=[smem, smem, vmem, anywhere, anywhere, anywhere, anywhere],
        out_specs=(vmem, vmem, vmem),
        scratch_shapes=[
            pltpu.VMEM((part, depth), jnp.bfloat16),
            pltpu.VMEM((height, rank_width), jnp.bfloat16),
            pltpu.VMEM((height, rank_width), jnp.bfloat16),
            pltpu.VMEM((height, width), jnp.float32),
            pltpu.VMEM((part, width), jnp.float32),
            pltpu.VMEM((cuts, part // cuts, width), jnp.bfloat16),
            pltpu.VMEM((rows, tiles, cuts, part // cuts, width), jnp.bfloat16),
            pltpu.VMEM((rank_width, width), jnp.float32),
            pltpu.VMEM((rank_width, width), jnp.float32),
            pltpu.SemaphoreType.DMA((4,)),
            pltpu.SemaphoreType.DMA,
            pltpu.SemaphoreType.DMA,
        ] + gather_sems(rows, cuts),
        compiler_params=pltpu.CompilerParams(
            collective_id=2 * step + 1, has_side_effects=True, vmem_limit_bytes=40 * 1024 * 1024),
        name="solve",
    )(pivots, ranks, pivot_block, diag, u_factor, v_factor, residual)


def local(rows, tiles, right_side, diag_inverse, u_factor, v_factor, ranks, pivots):
    current = right_side[0]
    residual = current.astype(jnp.float32)
    solved_list = []
    for step in range(PIVOTS):
        pivot_block = spread(rows, tiles, step, current, pivots)
        solved, residual, current = solve(
            rows, tiles, step, pivots, ranks, pivot_block, diag_inverse, u_factor, v_factor, residual)
        solved_list.append(solved)
    return (jnp.stack(solved_list), residual[None])


def solution(mesh):
    in_specs = (
        P(("grp", "row"), "tile", None),
        P(None, ("row", "tile"), None),
        P("row", None, "tile", None),
        P("row", None, "tile", None),
        P("row", None),
        P(),
    )
    out_specs = (P(None, ("grp", "row", "tile"), None), P(("grp", "row"), "tile", None))
    body = functools.partial(local, mesh.shape["row"], mesh.shape["tile"])
    return jax.shard_map(body, mesh=mesh, in_specs=in_specs, out_specs=out_specs, check_vma=False)
```

```python
import functools

import jax
import jax.numpy as jnp
from jax import lax
from jax.experimental import pallas as pl
from jax.experimental.pallas import tpu as pltpu
from jax.sharding import PartitionSpec as P

PIVOTS = 3
MESH = pl.DeviceIdType.MESH


class Place:
    def __init__(self, rows):
        self.rows = rows
        self.lanes = rows // 2
        self.grp = lax.axis_index("grp")
        self.row = lax.axis_index("row")
        self.tile = lax.axis_index("tile")
        self.side = lax.rem(self.row, 2)
        self.lane = lax.div(self.row, 2)

    def peer(self, offset):
        return lax.rem(self.lane + offset, self.lanes) * 2 + self.side

    def source(self, offset):
        return lax.rem(self.lane + self.lanes - offset, self.lanes) * 2 + self.side

    def across(self, row):
        return row + 1 - 2 * self.side

    def to(self, row, tile):
        return (self.grp, row, tile)


def greet(at):
    barrier = pltpu.get_barrier_semaphore()
    targets = [at.to(at.across(at.row), at.tile), at.to(at.row, 1 - at.tile)]
    targets += [at.to(at.peer(k), at.tile) for k in range(1, at.lanes)]
    for target in targets:
        pl.semaphore_signal(barrier, inc=1, device_id=target, device_id_type=MESH)
    pl.semaphore_wait(barrier, len(targets))


def each(low, high, body):
    def step(index, carry):
        body(index)
        return carry

    lax.fori_loop(low, high, step, 0)


def gather_body(at, cuts, src, out_at, sems, ready=None):
    z_right, z_left, z_recv, x_send, x_recv, t_send, t_recv = sems
    lane, last = at.lane, at.lanes - 1
    side_row = at.across(at.row)
    mate = 1 - at.tile

    def copy(source, slot, send_sem, recv_sem, target):
        return pltpu.make_async_remote_copy(
            src_ref=source, dst_ref=slot, send_sem=send_sem, recv_sem=recv_sem,
            device_id=target, device_id_type=MESH)

    def right(source, owner, cut):
        i = owner * cuts + cut
        return copy(source, out_at(owner * 2 + at.side, at.tile, cut), z_right.at[i], z_recv.at[i],
                    at.to(at.row + 2, at.tile))

    def left(source, owner, cut):
        i = owner * cuts + cut
        return copy(source, out_at(owner * 2 + at.side, at.tile, cut), z_left.at[i], z_recv.at[i],
                    at.to(at.row - 2, at.tile))

    def sidewards(source, owner, cut):
        i = owner * cuts + cut
        return copy(source, out_at(owner * 2 + at.side, at.tile, cut), x_send.at[i], x_recv.at[i],
                    at.to(side_row, at.tile))

    def to_mate(source, row, cut):
        i = row * cuts + cut
        return copy(source, out_at(row, at.tile, cut), t_send.at[i], t_recv.at[i], at.to(at.row, mate))

    def own_slot(owner, cut):
        return out_at(owner * 2 + at.side, at.tile, cut)

    def arrived(slot, sem):
        copy(slot, slot, t_send.at[0], sem, at.to(at.row, mate)).wait_recv()

    for cut in range(cuts):
        if ready is not None:
            ready(cut)

        @pl.when(lane < last)
        def _(cut=cut):
            right(src.at[cut], lane, cut).start()

        @pl.when(lane > 0)
        def _(cut=cut):
            left(src.at[cut], lane, cut).start()

        sidewards(src.at[cut], lane, cut).start()
        to_mate(src.at[cut], at.row, cut).start()
    for cut in range(cuts):
        own_slot(lane, cut)[...] = src[cut]

    def from_line(owner, cut):
        slot = own_slot(owner, cut)
        arrived(slot, z_recv.at[owner * cuts + cut])
        return slot

    def from_side(owner, cut):
        row = owner * 2 + 1 - at.side
        slot = out_at(row, at.tile, cut)
        arrived(slot, x_recv.at[owner * cuts + cut])
        to_mate(slot, row, cut).start()

    def side_arrivals(k):
        for cut in range(cuts):
            @pl.when(lane >= k)
            def _(cut=cut):
                from_side(lane - k, cut)

            @pl.when(jnp.logical_and(lane + k <= last, k > 0))
            def _(cut=cut):
                from_side(lane + k, cut)

    def hop(k):
        for cut in range(cuts):
            @pl.when(lane >= k)
            def _(cut=cut):
                slot = from_line(lane - k, cut)

                @pl.when(lane < last)
                def _():
                    right(slot, lane - k, cut).start()

                sidewards(slot, lane - k, cut).start()
                to_mate(slot, (lane - k) * 2 + at.side, cut).start()

            @pl.when(lane + k <= last)
            def _(cut=cut):
                slot = from_line(lane + k, cut)

                @pl.when(lane > 0)
                def _():
                    left(slot, lane + k, cut).start()

                sidewards(slot, lane + k, cut).start()
                to_mate(slot, (lane + k) * 2 + at.side, cut).start()
        side_arrivals(k - 1)

    each(1, at.lanes, hop)
    side_arrivals(last)

    def finish(owner):
        for cut in range(cuts):
            slot = own_slot(owner, cut)

            @pl.when(jnp.logical_and(owner <= lane, lane < last))
            def _(slot=slot, cut=cut):
                right(slot, owner, cut).wait_send()

            @pl.when(jnp.logical_and(owner >= lane, lane > 0))
            def _(slot=slot, cut=cut):
                left(slot, owner, cut).wait_send()

            sidewards(slot, owner, cut).wait_send()
            for side in range(2):
                row = owner * 2 + side
                arrived(out_at(row, mate, cut), t_recv.at[row * cuts + cut])
                to_mate(out_at(row, at.tile, cut), row, cut).wait_send()

    each(0, at.lanes, finish)


def cuts_of(part):
    return max(1, min(8, part // 16))


def gather_sems(rows, cuts):
    column = pltpu.SemaphoreType.DMA((rows // 2 * cuts,))
    whole = pltpu.SemaphoreType.DMA((rows * cuts,))
    return [column] * 5 + [whole] * 2


def indicator(condition):
    return jnp.where(condition, jnp.float32(1.0), jnp.float32(0.0))


def solve_kernel(rows, cuts, step, pivots, ranks, pivot_block, diag, u_hbm, v_hbm, residual,
                 solved, new_residual, current, diag_buf, u_buf, v_buf, res_buf, total, piece, full,
                 partial, other, load_sems, mate_send, mate_recv, *sems):
    at = Place(rows)
    part, width = solved.shape
    loads = [
        pltpu.make_async_copy(diag.at[step], diag_buf, load_sems.at[0]),
        pltpu.make_async_copy(v_hbm.at[0, step], v_buf, load_sems.at[1]),
        pltpu.make_async_copy(u_hbm.at[0, step], u_buf, load_sems.at[2]),
        pltpu.make_async_copy(residual, res_buf, load_sems.at[3]),
    ]
    for load in loads:
        load.start()
    greet(at)
    loads[0].wait()
    depth = diag_buf.shape[1]
    span = depth // 8
    total[...] = jnp.zeros_like(total)

    def product(i):
        k = pl.multiple_of(i * span, span)
        total[...] += jnp.dot(diag_buf[:, pl.ds(k, span)], pivot_block[pl.ds(k, span), :],
                              preferred_element_type=jnp.float32)

    each(0, 8, product)
    own = total[...].astype(jnp.bfloat16)
    solved[...] = own
    piece[...] = own.reshape(piece.shape)
    gather_body(at, cuts, piece, lambda row, tile, cut: full.at[row, tile, cut], sems)
    loads[1].wait()
    partial[...] = jnp.zeros_like(partial)
    lanes = at.lanes

    def inner(i):
        k = pl.multiple_of(i * part, part)
        values = full[at.tile * lanes + lax.div(i, 2), lax.rem(i, 2)].reshape(part, width)
        partial[...] += lax.dot_general(v_buf[pl.ds(k, part), :], values, (((0,), (0,)), ((), ())),
                                        preferred_element_type=jnp.float32)

    each(0, rows, inner)
    swap = pltpu.make_async_remote_copy(
        src_ref=partial, dst_ref=other, send_sem=mate_send, recv_sem=mate_recv,
        device_id=at.to(at.row, 1 - at.tile), device_id_type=MESH)
    swap.start()
    loads[2].wait()
    loads[3].wait()
    swap.wait()
    columns = lax.broadcasted_iota(jnp.int32, partial.shape, 0)
    coef = jnp.where(columns < ranks[0, step], partial[...] + other[...], jnp.float32(0.0))
    coef = coef.astype(jnp.bfloat16)
    keep = jnp.float32(1.0)
    for p in range(step + 1):
        keep = keep * indicator(pivots[p] != at.row)
    height = res_buf.shape[0]
    block = height // 8

    def outer(i):
        k = pl.ds(pl.multiple_of(i * block, block), block)
        update = jnp.dot(u_buf[k, :], coef, preferred_element_type=jnp.float32)
        value = res_buf[k, :] - update * keep
        new_residual[k, :] = value
        current[k, :] = value.astype(jnp.bfloat16)

    each(0, 8, outer)


def spread_kernel(rows, cuts, step, pivots, src, out, from_side, mixed, from_col, piece,
                  rs_sends, rs_side, rs_col, *sems):
    at = Place(rows)
    lanes = at.lanes
    greet(at)
    side_row = at.across(at.row)
    order = list(range(1, lanes)) + [0]
    side_copies = {}
    for cut in range(cuts):
        for k in order:
            i = cut * lanes + k
            copy = pltpu.make_async_remote_copy(
                src_ref=src.at[at.across(at.peer(k)), cut], dst_ref=from_side.at[i],
                send_sem=rs_sends.at[i], recv_sem=rs_side.at[i],
                device_id=at.to(side_row, at.tile), device_id_type=MESH)
            copy.start()
            side_copies[i] = copy
    root = pivots[step]
    own = indicator(root == at.row)
    root_lane = lax.div(root, 2)
    col_copies = {}

    def mix(cut):
        for k in order:
            i = cut * lanes + k
            side_copies[i].wait_recv()
            value = src[at.peer(k), cut].astype(jnp.float32) * own
            value = value + from_side[i].astype(jnp.float32) * (1.0 - own)
            mixed[i] = value.astype(jnp.bfloat16)
            if k:
                copy = pltpu.make_async_remote_copy(
                    src_ref=mixed.at[i], dst_ref=from_col.at[i],
                    send_sem=rs_sends.at[cuts * lanes + i], recv_sem=rs_col.at[i],
                    device_id=at.to(at.peer(k), at.tile), device_id_type=MESH)
                copy.start()
                col_copies[i] = copy

    def ready(cut):
        if cut == 0:
            mix(0)
        if cut + 1 < cuts:
            mix(cut + 1)
        total = mixed[cut * lanes].astype(jnp.float32) * indicator(root_lane == at.lane)
        for k in range(1, lanes):
            i = cut * lanes + k
            col_copies[i].wait_recv()
            total = total + from_col[i].astype(jnp.float32) * indicator(
                root_lane == lax.div(at.source(k), 2))
        piece[cut] = total.astype(jnp.bfloat16)

    gather_body(at, cuts, piece, lambda row, tile, cut: out.at[tile, row, cut], sems, ready)
    for copy in list(side_copies.values()) + list(col_copies.values()):
        copy.wait_send()


def spread(rows, tiles, step, current, pivots):
    half, width = current.shape
    part = half // rows
    lanes = rows // 2
    cuts = cuts_of(part)
    out = pl.pallas_call(
        functools.partial(spread_kernel, rows, cuts, step),
        out_shape=jax.ShapeDtypeStruct((tiles, rows, cuts, part // cuts, width), jnp.bfloat16),
        in_specs=[pl.BlockSpec(memory_space=pltpu.SMEM), pl.BlockSpec(memory_space=pltpu.VMEM)],
        out_specs=pl.BlockSpec(memory_space=pltpu.VMEM),
        scratch_shapes=[
            pltpu.VMEM((cuts * lanes, part // cuts, width), jnp.bfloat16),
            pltpu.VMEM((cuts * lanes, part // cuts, width), jnp.bfloat16),
            pltpu.VMEM((cuts * lanes, part // cuts, width), jnp.bfloat16),
            pltpu.VMEM((cuts, part // cuts, width), jnp.bfloat16),
            pltpu.SemaphoreType.DMA((2 * cuts * lanes,)),
            pltpu.SemaphoreType.DMA((cuts * lanes,)),
            pltpu.SemaphoreType.DMA((cuts * lanes,)),
        ] + gather_sems(rows, cuts),
        compiler_params=pltpu.CompilerParams(
            collective_id=2 * step, has_side_effects=True, vmem_limit_bytes=32 * 1024 * 1024),
        name="spread",
    )(pivots, current.reshape(rows, cuts, part // cuts, width))
    return out.reshape(tiles * half, width)


def solve(rows, tiles, step, pivots, ranks, pivot_block, diag, u_factor, v_factor, residual):
    part, depth = diag.shape[1:]
    height, width = residual.shape
    rank_width = u_factor.shape[3]
    cuts = cuts_of(part)
    smem = pl.BlockSpec(memory_space=pltpu.SMEM)
    vmem = pl.BlockSpec(memory_space=pltpu.VMEM)
    anywhere = pl.BlockSpec(memory_space=pl.ANY)
    return pl.pallas_call(
        functools.partial(solve_kernel, rows, cuts, step),
        out_shape=(
            jax.ShapeDtypeStruct((part, width), jnp.bfloat16),
            jax.ShapeDtypeStruct((height, width), jnp.float32),
            jax.ShapeDtypeStruct((height, width), jnp.bfloat16),
        ),
        in_specs=[smem, smem, vmem, anywhere, anywhere, anywhere, anywhere],
        out_specs=(vmem, vmem, vmem),
        scratch_shapes=[
            pltpu.VMEM((part, depth), jnp.bfloat16),
            pltpu.VMEM((height, rank_width), jnp.bfloat16),
            pltpu.VMEM((height, rank_width), jnp.bfloat16),
            pltpu.VMEM((height, width), jnp.float32),
            pltpu.VMEM((part, width), jnp.float32),
            pltpu.VMEM((cuts, part // cuts, width), jnp.bfloat16),
            pltpu.VMEM((rows, tiles, cuts, part // cuts, width), jnp.bfloat16),
            pltpu.VMEM((rank_width, width), jnp.float32),
            pltpu.VMEM((rank_width, width), jnp.float32),
            pltpu.SemaphoreType.DMA((4,)),
            pltpu.SemaphoreType.DMA,
            pltpu.SemaphoreType.DMA,
        ] + gather_sems(rows, cuts),
        compiler_params=pltpu.CompilerParams(
            collective_id=2 * step + 1, has_side_effects=True, vmem_limit_bytes=40 * 1024 * 1024),
        name="solve",
    )(pivots, ranks, pivot_block, diag, u_factor, v_factor, residual)


def local(rows, tiles, right_side, diag_inverse, u_factor, v_factor, ranks, pivots):
    current = right_side[0]
    residual = current.astype(jnp.float32)
    solved_list = []
    for step in range(PIVOTS):
        pivot_block = spread(rows, tiles, step, current, pivots)
        solved, residual, current = solve(
            rows, tiles, step, pivots, ranks, pivot_block, diag_inverse, u_factor, v_factor, residual)
        solved_list.append(solved)
    return (jnp.stack(solved_list), residual[None])


def solution(mesh):
    in_specs = (
        P(("grp", "row"), "tile", None),
        P(None, ("row", "tile"), None),
        P("row", None, "tile", None),
        P("row", None, "tile", None),
        P("row", None),
        P(),
    )
    out_specs = (P(None, ("grp", "row", "tile"), None), P(("grp", "row"), "tile", None))
    body = functools.partial(local, mesh.shape["row"], mesh.shape["tile"])
    return jax.shard_map(body, mesh=mesh, in_specs=in_specs, out_specs=out_specs, check_vma=False)
```
